512 devices in a mesh: segment: 8 (over x_hi, y), seq: 64 (over x_lo, z, core).
Axes of the slice: x: 4 (x_hi: 2, x_lo: 2; x = x_hi * 2 + x_lo), y: 4, z: 16, core: 2. Of those that a mesh axis runs over, the one named last changes fastest.
Arguments:
- query_rows: bfloat16 [8, 12288, 1536], P('segment', 'seq'), may hold values from -10 to 10
- key_rows: bfloat16 [8, 12288, 1536], P('segment', 'seq'), may hold values from -10 to 10
- value_rows: bfloat16 [8, 12288, 1536], P('segment', 'seq'), may hold values from -6 to 6
- handoff: bfloat16 [8, 12288, 1536], P('segment', 'seq'), may hold values from -6 to 6
Outputs:
- grad_query: bfloat16 [8, 12288, 1536], P('segment', 'seq')
- grad_key: bfloat16 [8, 12288, 1536], P('segment', 'seq')
- grad_value: bfloat16 [8, 12288, 1536], P('segment', 'seq')
The draws below stay inside these ranges and needn't reach their ends.
All inputs are finite; a program needn't handle non-finite values.
Results may differ from the reference program's by a relative error of at most 0.0091.
Values may be sent and summed in bfloat16 or wider, within the bound.
A program may use at most 64 MiB of HBM per device.

```python
import jax
import jax.numpy as jnp
from jax import lax

HEAD = 128
HALF = 6
SECTIONS = 8
FRAMES = 32
POS = 384
TOKENS = 12288
WIDTH = 1536


def draw_query_rows(key, part):
    key = jax.random.fold_in(key, 11)
    full_shape = (SECTIONS, TOKENS, WIDTH)
    base_draw = 1.5 * jnp.clip(jax.random.normal(key, full_shape, jnp.float32), -6.0, 6.0)
    return base_draw.astype(jnp.bfloat16)


def draw_key_rows(key, part):
    key = jax.random.fold_in(key, 23)
    full_shape = (SECTIONS, TOKENS, WIDTH)
    base_draw = 1.5 * jnp.clip(jax.random.normal(key, full_shape, jnp.float32), -6.0, 6.0)
    return base_draw.astype(jnp.bfloat16)


def block_scale(rng, extent, pieces, smallest, high):
    level, own = 1.0, jax.random.fold_in(rng, 6)
    for position, blocks in pieces:
        steps = jnp.exp(jax.random.uniform(jax.random.fold_in(own, position), (blocks,), jnp.float32, smallest / len(pieces), high / len(pieces)))
        level = level * jnp.repeat(steps, extent[position] // blocks).reshape([-1 if axis == position else 1 for axis in range(len(extent))])
    return level


def centred(rng, dims, deviation, bound, shards=(), held_as=jnp.bfloat16):
    entries = jax.random.normal(rng, dims, jnp.float32) * deviation
    if len(shards) > 0:
        entries = block_scale(rng, dims, shards, -0.22, 0.18) * entries
    return jnp.clip(entries, min=-bound, max=bound).astype(held_as)


def setup_inputs(seed: int = 0) -> dict:
    splits = jax.random.split(jax.random.key(seed), 5)
    query_rows = draw_query_rows(jax.random.fold_in(splits[4], 71), 0)
    key_rows = draw_key_rows(jax.random.fold_in(splits[4], 71), 0)
    value_rows = centred(splits[2], (SECTIONS, TOKENS, WIDTH), 1.0, 6.0, ((0, 8), (1, 64)))
    handoff = centred(splits[3], (SECTIONS, TOKENS, WIDTH), 1.0, 6.0, ((0, 8), (1, 64)))
    return dict(query_rows=query_rows, key_rows=key_rows, value_rows=value_rows, handoff=handoff)


def head_backward(query_matrix, key_portion, value_portion, output_gradient):
    scale_factor = HEAD ** -0.5
    scores = jnp.dot(query_matrix, key_portion.T, preferred_element_type=jnp.float32) * scale_factor
    highest = jnp.max(scores, axis=-1, keepdims=True)
    log_total = highest + jnp.log(jnp.sum(jnp.exp(scores - highest), axis=-1, keepdims=True))
    weights = jnp.exp(scores - log_total)
    lower_weights = weights.astype(jnp.bfloat16)
    outputs = jnp.dot(lower_weights, value_portion, preferred_element_type=jnp.float32)
    row_delta = jnp.sum(output_gradient.astype(jnp.float32) * outputs, axis=-1, keepdims=True)
    grad_values = jnp.dot(lower_weights.T, output_gradient, preferred_element_type=jnp.float32)
    grad_weights = jnp.dot(output_gradient, value_portion.T, preferred_element_type=jnp.float32)
    score_gradient = (weights * (grad_weights - row_delta)).astype(jnp.bfloat16)
    grad_queries = jnp.dot(score_gradient, key_portion, preferred_element_type=jnp.float32) * scale_factor
    grad_keys = jnp.dot(score_gradient.T, query_matrix, preferred_element_type=jnp.float32) * scale_factor
    return grad_queries.astype(jnp.bfloat16), grad_keys.astype(jnp.bfloat16), grad_values.astype(jnp.bfloat16)


def spatial_form(array):
    spatial_width = HALF * HEAD
    return array[:, :spatial_width].reshape(FRAMES, POS, HALF, HEAD).transpose(0, 2, 1, 3).reshape(FRAMES * HALF, POS, HEAD)


def temporal_form(array):
    spatial_width = HALF * HEAD
    return array[:, spatial_width:].reshape(FRAMES, POS, HALF, HEAD).transpose(1, 2, 0, 3).reshape(POS * HALF, FRAMES, HEAD)


def spatial_back(array):
    return array.reshape(FRAMES, HALF, POS, HEAD).transpose(0, 2, 1, 3).reshape(TOKENS, HALF * HEAD)


def temporal_back(array):
    return array.reshape(POS, HALF, FRAMES, HEAD).transpose(2, 0, 1, 3).reshape(TOKENS, HALF * HEAD)


def section_backward(operands):
    spatial_in = tuple(spatial_form(member) for member in operands)
    temporal_in = tuple(temporal_form(member) for member in operands)
    spatial = lax.map(lambda group: head_backward(group[0], group[1], group[2], group[3]), spatial_in)
    temporal = jax.vmap(head_backward)(temporal_in[0], temporal_in[1], temporal_in[2], temporal_in[3])
    return tuple(jnp.concatenate([spatial_back(first), temporal_back(second)], axis=1) for first, second in zip(spatial, temporal))


def reference(query_rows, key_rows, value_rows, handoff):
    output_gradient = jnp.roll(handoff, -1, axis=0)
    results = lax.map(section_backward, (query_rows, key_rows, value_rows, output_gradient))
    return (results[0], results[1], results[2])
```

```python
import jax
import jax.numpy as jnp
from jax import lax
from jax.experimental import pallas as pl
from jax.experimental.pallas import tpu as pltpu
from jax.sharding import PartitionSpec as P

MESH = pl.DeviceIdType.MESH
HEAD = 128
HALF = 6
ROWS = 192
SIDE = HALF * HEAD
UNIT = 16
CHIPS = 32
RING = 16
UNITS = ROWS // UNIT * HALF
EXTRA = UNITS - 2 * CHIPS
SCALE = HEAD**-0.5
BF16, F32 = jnp.bfloat16, jnp.float32


def dot_nt(a, b):
    return lax.dot_general(a, b, (((1,), (1,)), ((), ())), preferred_element_type=F32)


def dot_tn(a, b):
    return lax.dot_general(a, b, (((0,), (0,)), ((), ())), preferred_element_type=F32)


def dot_nn(a, b):
    return lax.dot_general(a, b, (((1,), (0,)), ((), ())), preferred_element_type=F32)


def attention_backward(q, k, v, g, mask):
    scores = dot_nt(q, k) * SCALE
    if mask is not None:
        scores = jnp.where(mask, scores, -jnp.inf)
    top = jnp.max(scores, axis=1, keepdims=True)
    raised = jnp.exp(scores - top)
    weights = raised * (1.0 / jnp.sum(raised, axis=1, keepdims=True))
    low = weights.astype(BF16)
    grad_weights = dot_nt(g, v)
    delta = jnp.sum(low.astype(F32) * grad_weights, axis=1, keepdims=True)
    grad_scores = (weights * (grad_weights - delta)).astype(BF16)
    dq = dot_nn(grad_scores, k) * SCALE
    dk = dot_tn(grad_scores, q) * SCALE
    dv = dot_tn(low, g)
    return dq, dk, dv


def kernel(
    q_hbm, k_hbm, v_hbm, h_hbm, dq_hbm, dk_hbm, dv_hbm,
    qs, kb, vb, gs, xt, gt, pack, gpack, inb, ing, outb, ret, own, sib_out, sib_in, acc, stage,
    load_sem, hand_send, hand_recv, pair_send, pair_recv, back_send, back_recv,
    in_send, in_recv, g_send, g_recv, out_send, out_recv, store_sem,
):
    seg = lax.axis_index("segment")
    me = lax.axis_index("seq")
    core = me % 2
    chip = me // 2
    z, xl = chip % RING, chip // RING
    sections = lax.axis_size("segment")
    seg_up = (seg + 1) % sections
    seg_down = (seg + sections - 1) % sections
    sibling = chip * 2 + (1 - core)
    has_extra = z % 4 == xl + 2 * core
    extra_slot = xl * 4 + z // 4

    def chip_at(o):
        dx, step = o % 2, o // 2
        dz = jnp.where(step % 2 == 1, (step + 1) // 2, RING - step // 2)
        return ((xl + dx) % 2) * RING + (z + dz) % RING

    loads = []
    for a, ref in enumerate((q_hbm, k_hbm, v_hbm)):
        loads.append(pltpu.make_async_copy(ref.at[:, SIDE:], xt.at[a], load_sem.at[a]))
    loads.append(pltpu.make_async_copy(k_hbm.at[:, :SIDE], kb.at[0], load_sem.at[3]))
    loads.append(pltpu.make_async_copy(v_hbm.at[:, :SIDE], vb.at[0], load_sem.at[4]))
    loads.append(pltpu.make_async_copy(q_hbm.at[:, :SIDE], qs, load_sem.at[5]))
    for load in loads:
        load.start()

    barrier = pltpu.get_barrier_semaphore()

    def greet(i, carry):
        pl.semaphore_signal(
            barrier, inc=1, device_id={"seq": chip_at(CHIPS - i) * 2 + core}, device_id_type=MESH
        )
        return carry

    lax.fori_loop(1, CHIPS, greet, 0)
    pl.semaphore_signal(barrier, inc=1, device_id={"segment": seg_up}, device_id_type=MESH)
    pl.semaphore_signal(barrier, inc=1, device_id={"seq": sibling}, device_id_type=MESH)

    for load in loads[:3]:
        load.wait()
    for n in range(UNITS):
        rows = slice(n // HALF * UNIT, (n // HALF + 1) * UNIT)
        cols = slice(n % HALF * HEAD, (n % HALF + 1) * HEAD)
        for a in range(3):
            pack[n, a] = xt[a, rows, cols]
    for load in loads[3:]:
        load.wait()

    pl.semaphore_wait(barrier, CHIPS + 1)

    hand_t = pltpu.make_async_remote_copy(
        h_hbm.at[:, SIDE:], gt, hand_send.at[0], hand_recv.at[0],
        device_id={"segment": seg_down}, device_id_type=MESH,
    )
    hand_s = pltpu.make_async_remote_copy(
        h_hbm.at[:, :SIDE], gs, hand_send.at[1], hand_recv.at[1],
        device_id={"segment": seg_down}, device_id_type=MESH,
    )
    hand_t.start()

    def send_in(u, source, landing, send, recv):
        pltpu.make_async_copy(source.at[u * CHIPS + chip], landing.at[u, chip], recv.at[u]).start()

        def one(o, carry):
            j = chip_at(o)
            pltpu.make_async_remote_copy(
                source.at[u * CHIPS + j], landing.at[u, chip], send.at[u], recv.at[u],
                device_id={"seq": j * 2 + core}, device_id_type=MESH,
            ).start()
            return carry

        lax.fori_loop(1, CHIPS, one, 0)

    def send_extra(source, landing, send, recv):
        def one(i, carry):
            col, quarter = i % 2, (z // 4 + i // 2) % 4
            j = col * RING + quarter * 4 + col + 2 * core
            slot = 2 * CHIPS + col * 4 + quarter

            @pl.when(j != chip)
            def _():
                pltpu.make_async_remote_copy(
                    source.at[slot], landing.at[2, chip], send.at[2], recv.at[2],
                    device_id={"seq": j * 2 + core}, device_id_type=MESH,
                ).start()

            @pl.when(j == chip)
            def _():
                pltpu.make_async_copy(source.at[slot], landing.at[2, chip], recv.at[2]).start()

            return carry

        lax.fori_loop(0, EXTRA, one, 0)

    def wait_bytes(ref, sem):
        pltpu.make_async_copy(ref, ref, sem).wait()

    send_in(0, pack, inb, in_send, in_recv)

    pair = []
    for a, buf in enumerate((kb, vb)):
        pair.append(
            pltpu.make_async_remote_copy(
                buf.at[0], buf.at[1], pair_send.at[a], pair_recv.at[a],
                device_id={"seq": sibling}, device_id_type=MESH,
            )
        )
        pair[-1].start()
    hand_s.start()

    hand_t.wait_recv()
    for n in range(UNITS):
        rows = slice(n // HALF * UNIT, (n // HALF + 1) * UNIT)
        cols = slice(n % HALF * HEAD, (n % HALF + 1) * HEAD)
        gpack[n] = gt[rows, cols]
    send_in(0, gpack, ing, g_send, g_recv)
    send_in(1, pack, inb, in_send, in_recv)
    send_in(1, gpack, ing, g_send, g_recv)
    send_extra(pack, inb, in_send, in_recv)
    send_extra(gpack, ing, g_send, g_recv)

    hand_s.wait_recv()
    for copy in pair:
        copy.wait_recv()

    for h in range(HALF):
        cols = slice(h * HEAD, (h + 1) * HEAD)
        k = kb[:, :, cols].reshape(2 * ROWS, HEAD)
        v = vb[:, :, cols].reshape(2 * ROWS, HEAD)
        dq, dk, dv = attention_backward(qs[:, cols], k, v, gs[:, cols], None)
        stage[0, :, cols] = dq.astype(BF16)
        own[0, :, cols] = dk[:ROWS]
        own[1, :, cols] = dv[:ROWS]
        sib_out[0, :, cols] = dk[ROWS:].astype(BF16)
        sib_out[1, :, cols] = dv[ROWS:].astype(BF16)
    back = pltpu.make_async_remote_copy(
        sib_out, sib_in, back_send, back_recv, device_id={"seq": sibling}, device_id_type=MESH
    )
    back.start()

    def temporal(u):
        wait_bytes(inb.at[u], in_recv.at[u])
        wait_bytes(ing.at[u], g_recv.at[u])
        k = inb[u, :, 1].reshape(CHIPS * UNIT, HEAD)
        v = inb[u, :, 2].reshape(CHIPS * UNIT, HEAD)
        part = CHIPS // 2
        row = lax.broadcasted_iota(jnp.int32, (part * UNIT, CHIPS * UNIT), 0)
        column = lax.broadcasted_iota(jnp.int32, (part * UNIT, CHIPS * UNIT), 1)
        mask = row % UNIT == column % UNIT
        for c in range(2):
            frames = slice(c * part, (c + 1) * part)
            q = inb[u, frames, 0].reshape(part * UNIT, HEAD)
            g = ing[u, frames].reshape(part * UNIT, HEAD)
            dq, dk, dv = attention_backward(q, k, v, g, mask)
            outb[u, frames, 0] = dq.astype(BF16).reshape(part, UNIT, HEAD)
            if c == 0:
                acc[0] = dk
                acc[1] = dv
            else:
                outb[u, :, 1] = (acc[0] + dk).astype(BF16).reshape(CHIPS, UNIT, HEAD)
                outb[u, :, 2] = (acc[1] + dv).astype(BF16).reshape(CHIPS, UNIT, HEAD)

        n = jnp.where(u < 2, u * CHIPS + chip, 2 * CHIPS + extra_slot)
        pltpu.make_async_copy(outb.at[u, chip], ret.at[n], out_recv.at[u]).start()

        def one(o, carry):
            j = chip_at(o)
            pltpu.make_async_remote_copy(
                outb.at[u, j], ret.at[n], out_send.at[u], out_recv.at[u],
                device_id={"seq": j * 2 + core}, device_id_type=MESH,
            ).start()
            return carry

        lax.fori_loop(1, CHIPS, one, 0)

    def rounds(u, carry):
        @pl.when(jnp.logical_or(u < 2, has_extra))
        def _():
            temporal(u)

        return carry

    lax.fori_loop(0, 3, rounds, 0)

    back.wait_recv()
    for a in range(2):
        stage[1 + a, :, :SIDE] = (own[a] + sib_in[a].astype(F32)).astype(BF16)
    stores = []
    for a, ref in enumerate((dq_hbm, dk_hbm, dv_hbm)):
        stores.append(
            pltpu.make_async_copy(stage.at[a, :, :SIDE], ref.at[:, :SIDE], store_sem.at[a])
        )
        stores[-1].start()

    for u, (first, last) in enumerate(((0, CHIPS), (CHIPS, 2 * CHIPS), (2 * CHIPS, UNITS))):
        wait_bytes(ret.at[first:last], out_recv.at[u])
        for n in range(first, last):
            rows = slice(n // HALF * UNIT, (n // HALF + 1) * UNIT)
            cols = slice(SIDE + n % HALF * HEAD, SIDE + (n % HALF + 1) * HEAD)
            for a in range(3):
                stage[a, rows, cols] = ret[n, a]
    for a, ref in enumerate((dq_hbm, dk_hbm, dv_hbm)):
        stores.append(
            pltpu.make_async_copy(stage.at[a, :, SIDE:], ref.at[:, SIDE:], store_sem.at[3 + a])
        )
        stores[-1].start()

    hand_t.wait_send()
    hand_s.wait_send()
    for copy in pair:
        copy.wait_send()
    back.wait_send()
    for u in range(2):
        wait_bytes(pack.at[: CHIPS - 1], in_send.at[u])
        wait_bytes(gpack.at[: CHIPS - 1], g_send.at[u])
        wait_bytes(outb.at[0, : CHIPS - 1], out_send.at[u])

    @pl.when(has_extra)
    def _():
        wait_bytes(pack.at[: EXTRA - 1], in_send.at[2])
        wait_bytes(gpack.at[: EXTRA - 1], g_send.at[2])
        wait_bytes(outb.at[0, : CHIPS - 1], out_send.at[2])

    @pl.when(jnp.logical_not(has_extra))
    def _():
        wait_bytes(pack.at[:EXTRA], in_send.at[2])
        wait_bytes(gpack.at[:EXTRA], g_send.at[2])

    for store in stores:
        store.wait()


def on_device(query_rows, key_rows, value_rows, handoff):
    shape = (ROWS, 2 * SIDE)
    dma = pltpu.SemaphoreType.DMA
    grads = pl.pallas_call(
        kernel,
        out_shape=[jax.ShapeDtypeStruct(shape, BF16)] * 3,
        in_specs=[pl.BlockSpec(memory_space=pl.ANY)] * 4,
        out_specs=[pl.BlockSpec(memory_space=pl.ANY)] * 3,
        scratch_shapes=[
            pltpu.VMEM((ROWS, SIDE), BF16),
            pltpu.VMEM((2, ROWS, SIDE), BF16),
            pltpu.VMEM((2, ROWS, SIDE), BF16),
            pltpu.VMEM((ROWS, SIDE), BF16),
            pltpu.VMEM((3, ROWS, SIDE), BF16),
            pltpu.VMEM((ROWS, SIDE), BF16),
            pltpu.VMEM((UNITS, 3, UNIT, HEAD), BF16),
            pltpu.VMEM((UNITS, UNIT, HEAD), BF16),
            pltpu.VMEM((3, CHIPS, 3, UNIT, HEAD), BF16),
            pltpu.VMEM((3, CHIPS, UNIT, HEAD), BF16),
            pltpu.VMEM((3, CHIPS, 3, UNIT, HEAD), BF16),
            pltpu.VMEM((UNITS, 3, UNIT, HEAD), BF16),
            pltpu.VMEM((2, ROWS, SIDE), F32),
            pltpu.VMEM((2, ROWS, SIDE), BF16),
            pltpu.VMEM((2, ROWS, SIDE), BF16),
            pltpu.VMEM((2, CHIPS * UNIT, HEAD), F32),
            pltpu.VMEM((3, ROWS, 2 * SIDE), BF16),
            dma((6,)),
            dma((2,)),
            dma((2,)),
            dma((2,)),
            dma((2,)),
            dma(()),
            dma(()),
            dma((3,)),
            dma((3,)),
            dma((3,)),
            dma((3,)),
            dma((3,)),
            dma((3,)),
            dma((6,)),
        ],
        compiler_params=pltpu.CompilerParams(
            collective_id=0, has_side_effects=True, vmem_limit_bytes=40 * 2**20
        ),
        name="space_time_backward",
    )(query_rows[0], key_rows[0], value_rows[0], handoff[0])
    return tuple(grad[None] for grad in grads)


def solution(mesh):
    spec = P("segment", "seq", None)
    return jax.shard_map(
        on_device, mesh=mesh, in_specs=(spec,) * 4, out_specs=(spec,) * 3, check_vma=False
    )
```

```python
import jax
import jax.numpy as jnp
from jax import lax
from jax.experimental import pallas as pl
from jax.experimental.pallas import tpu as pltpu
from jax.sharding import PartitionSpec as P

MESH = pl.DeviceIdType.MESH
HEAD = 128
HALF = 6
ROWS = 192
SIDE = HALF * HEAD
UNIT = 16
CHIPS = 32
RING = 16
UNITS = ROWS // UNIT * HALF
EXTRA = UNITS - 2 * CHIPS
SCALE = HEAD**-0.5
BF16, F32 = jnp.bfloat16, jnp.float32


def dot_nt(a, b):
    return lax.dot_general(a, b, (((1,), (1,)), ((), ())), preferred_element_type=F32)


def dot_tn(a, b):
    return lax.dot_general(a, b, (((0,), (0,)), ((), ())), preferred_element_type=F32)


def dot_nn(a, b):
    return lax.dot_general(a, b, (((1,), (0,)), ((), ())), preferred_element_type=F32)


def attention_backward(q, k, v, g, mask):
    scores = dot_nt(q, k) * SCALE
    if mask is not None:
        scores = jnp.where(mask, scores, -jnp.inf)
    top = jnp.max(scores, axis=1, keepdims=True)
    raised = jnp.exp(scores - top)
    weights = raised * (1.0 / jnp.sum(raised, axis=1, keepdims=True))
    low = weights.astype(BF16)
    grad_weights = dot_nt(g, v)
    delta = jnp.sum(low.astype(F32) * grad_weights, axis=1, keepdims=True)
    grad_scores = (weights * (grad_weights - delta)).astype(BF16)
    dq = dot_nn(grad_scores, k) * SCALE
    dk = dot_tn(grad_scores, q) * SCALE
    dv = dot_tn(low, g)
    return dq, dk, dv


def kernel(
    q_hbm, k_hbm, v_hbm, h_hbm, grads,
    qs, kb, vb, gs, xt, gt, pack, gpack, inb, ing, outb, own, sib_out, sib_in, acc, stage,
    load_sem, hand_send, hand_recv, pair_send, pair_recv, back_send, back_recv,
    in_send, in_recv, g_send, g_recv, out_send, out_recv, store_sem,
):
    seg = lax.axis_index("segment")
    me = lax.axis_index("seq")
    core = me % 2
    chip = me // 2
    z, xl = chip % RING, chip // RING
    sections = lax.axis_size("segment")
    seg_up = (seg + 1) % sections
    seg_down = (seg + sections - 1) % sections
    sibling = chip * 2 + (1 - core)
    has_extra = z % 4 == xl + 2 * core
    extra_slot = xl * 4 + z // 4

    def chip_at(o):
        dx, step = o % 2, o // 2
        dz = jnp.where(step % 2 == 1, (step + 1) // 2, RING - step // 2)
        return ((xl + dx) % 2) * RING + (z + dz) % RING

    loads = []
    for a, ref in enumerate((q_hbm, k_hbm, v_hbm)):
        loads.append(pltpu.make_async_copy(ref.at[:, SIDE:], xt.at[a], load_sem.at[a]))
    loads.append(pltpu.make_async_copy(k_hbm.at[:, :SIDE], kb.at[0], load_sem.at[3]))
    loads.append(pltpu.make_async_copy(v_hbm.at[:, :SIDE], vb.at[0], load_sem.at[4]))
    loads.append(pltpu.make_async_copy(q_hbm.at[:, :SIDE], qs, load_sem.at[5]))
    for load in loads[:3]:
        load.start()

    barrier = pltpu.get_barrier_semaphore()

    def greet(i, carry):
        pl.semaphore_signal(
            barrier, inc=1, device_id={"seq": chip_at(CHIPS - i) * 2 + core}, device_id_type=MESH
        )
        return carry

    lax.fori_loop(1, CHIPS, greet, 0, unroll=True)
    pl.semaphore_signal(barrier, inc=1, device_id={"segment": seg_up}, device_id_type=MESH)
    pl.semaphore_signal(barrier, inc=1, device_id={"seq": sibling}, device_id_type=MESH)
    for load in loads[3:]:
        load.start()

    for load in loads[:3]:
        load.wait()
    for n in range(UNITS):
        rows = slice(n // HALF * UNIT, (n // HALF + 1) * UNIT)
        cols = slice(n % HALF * HEAD, (n % HALF + 1) * HEAD)
        for a in range(3):
            pack[n, a] = xt[a, rows, cols]
    for load in loads[3:]:
        load.wait()

    pl.semaphore_wait(barrier, CHIPS + 1)

    hand_t = pltpu.make_async_remote_copy(
        h_hbm.at[:, SIDE:], gt, hand_send.at[0], hand_recv.at[0],
        device_id={"segment": seg_down}, device_id_type=MESH,
    )
    hand_s = pltpu.make_async_remote_copy(
        h_hbm.at[:, :SIDE], gs, hand_send.at[1], hand_recv.at[1],
        device_id={"segment": seg_down}, device_id_type=MESH,
    )
    hand_t.start()

    def send_in(u, source, landing, send, recv):
        pltpu.make_async_copy(source.at[u * CHIPS + chip], landing.at[u, chip], recv.at[u]).start()

        def one(o, carry):
            j = chip_at(o)
            pltpu.make_async_remote_copy(
                source.at[u * CHIPS + j], landing.at[u, chip], send.at[u], recv.at[u],
                device_id={"seq": j * 2 + core}, device_id_type=MESH,
            ).start()
            return carry

        lax.fori_loop(1, CHIPS, one, 0)

    def send_extra(source, landing, send, recv):
        def one(i, carry):
            col, quarter = i % 2, (z // 4 + i // 2) % 4
            j = col * RING + quarter * 4 + col + 2 * core
            slot = 2 * CHIPS + col * 4 + quarter

            @pl.when(j != chip)
            def _():
                pltpu.make_async_remote_copy(
                    source.at[slot], landing.at[2, chip], send.at[2], recv.at[2],
                    device_id={"seq": j * 2 + core}, device_id_type=MESH,
                ).start()

            @pl.when(j == chip)
            def _():
                pltpu.make_async_copy(source.at[slot], landing.at[2, chip], recv.at[2]).start()

            return carry

        lax.fori_loop(0, EXTRA, one, 0)

    def wait_bytes(ref, sem):
        pltpu.make_async_copy(ref, ref, sem).wait()

    send_in(0, pack, inb, in_send, in_recv)

    pair = []
    for a, buf in enumerate((kb, vb)):
        pair.append(
            pltpu.make_async_remote_copy(
                buf.at[0], buf.at[1], pair_send.at[a], pair_recv.at[a],
                device_id={"seq": sibling}, device_id_type=MESH,
            )
        )
        pair[-1].start()
    hand_s.start()

    hand_t.wait_recv()
    for n in range(UNITS):
        rows = slice(n // HALF * UNIT, (n // HALF + 1) * UNIT)
        cols = slice(n % HALF * HEAD, (n % HALF + 1) * HEAD)
        gpack[n] = gt[rows, cols]
    send_in(0, gpack, ing, g_send, g_recv)
    send_in(1, pack, inb, in_send, in_recv)
    send_in(1, gpack, ing, g_send, g_recv)
    send_extra(pack, inb, in_send, in_recv)
    send_extra(gpack, ing, g_send, g_recv)

    hand_s.wait_recv()
    for copy in pair:
        copy.wait_recv()

    for h in range(HALF):
        cols = slice(h * HEAD, (h + 1) * HEAD)
        k = kb[:, :, cols].reshape(2 * ROWS, HEAD)
        v = vb[:, :, cols].reshape(2 * ROWS, HEAD)
        dq, dk, dv = attention_backward(qs[:, cols], k, v, gs[:, cols], None)
        stage[0, :, cols] = dq.astype(BF16)
        own[0, :, cols] = dk[:ROWS]
        own[1, :, cols] = dv[:ROWS]
        sib_out[0, :, cols] = dk[ROWS:].astype(BF16)
        sib_out[1, :, cols] = dv[ROWS:].astype(BF16)
    back = pltpu.make_async_remote_copy(
        sib_out, sib_in, back_send, back_recv, device_id={"seq": sibling}, device_id_type=MESH
    )
    back.start()

    def temporal(u):
        wait_bytes(inb.at[u], in_recv.at[u])
        wait_bytes(ing.at[u], g_recv.at[u])
        k = inb[u, :, 1].reshape(CHIPS * UNIT, HEAD)
        v = inb[u, :, 2].reshape(CHIPS * UNIT, HEAD)
        part = CHIPS // 2
        row = lax.broadcasted_iota(jnp.int32, (part * UNIT, CHIPS * UNIT), 0)
        column = lax.broadcasted_iota(jnp.int32, (part * UNIT, CHIPS * UNIT), 1)
        mask = row % UNIT == column % UNIT
        for c in range(2):
            frames = slice(c * part, (c + 1) * part)
            q = inb[u, frames, 0].reshape(part * UNIT, HEAD)
            g = ing[u, frames].reshape(part * UNIT, HEAD)
            dq, dk, dv = attention_backward(q, k, v, g, mask)
            outb[u, frames, 0] = dq.astype(BF16).reshape(part, UNIT, HEAD)
            if c == 0:
                acc[0] = dk
                acc[1] = dv
            else:
                outb[u, :, 1] = (acc[0] + dk).astype(BF16).reshape(CHIPS, UNIT, HEAD)
                outb[u, :, 2] = (acc[1] + dv).astype(BF16).reshape(CHIPS, UNIT, HEAD)

        pltpu.make_async_copy(outb.at[u, chip], home(u), out_recv.at[u]).start()

    def home(u):
        n = jnp.where(u < 2, u * CHIPS + chip, 2 * CHIPS + extra_slot)
        rows = pl.ds(pl.multiple_of(n // HALF * UNIT, UNIT), UNIT)
        cols = pl.ds(pl.multiple_of(SIDE + n % HALF * HEAD, HEAD), HEAD)
        return grads.at[:, rows, cols]

    def send_out(u, base, count):
        landing = home(u)

        def one(i, carry):
            j = (xl + i) % 2 * RING + base + (z + i // 2) % count

            @pl.when(j != chip)
            def _():
                pltpu.make_async_remote_copy(
                    outb.at[u, j], landing, out_send.at[u], out_recv.at[u],
                    device_id={"seq": j * 2 + core}, device_id_type=MESH,
                ).start()

            return carry

        lax.fori_loop(0, 2 * count, one, 0)

    early, middle, late = (0, 4), (4, 4), (8, 8)
    temporal(0)
    for where in (early, middle, late):
        send_out(0, *where)
    temporal(1)
    send_out(1, *early)

    @pl.when(has_extra)
    def _():
        temporal(2)
        send_out(2, *early)

    send_out(1, *middle)

    @pl.when(has_extra)
    def _():
        send_out(2, *middle)

    send_out(1, *late)

    @pl.when(has_extra)
    def _():
        send_out(2, *late)

    back.wait_recv()
    for a in range(2):
        stage[1 + a] = (own[a] + sib_in[a].astype(F32)).astype(BF16)
    store = pltpu.make_async_copy(stage, grads.at[:, :, :SIDE], store_sem)
    store.start()

    for u in range(2):
        wait_bytes(outb.at[0], out_recv.at[u])
    wait_bytes(outb.at[0, :EXTRA], out_recv.at[2])

    hand_t.wait_send()
    hand_s.wait_send()
    for copy in pair:
        copy.wait_send()
    back.wait_send()
    for u in range(2):
        wait_bytes(pack.at[: CHIPS - 1], in_send.at[u])
        wait_bytes(gpack.at[: CHIPS - 1], g_send.at[u])
        wait_bytes(outb.at[0, : CHIPS - 1], out_send.at[u])

    @pl.when(has_extra)
    def _():
        wait_bytes(pack.at[: EXTRA - 1], in_send.at[2])
        wait_bytes(gpack.at[: EXTRA - 1], g_send.at[2])
        wait_bytes(outb.at[0, : CHIPS - 1], out_send.at[2])

    @pl.when(jnp.logical_not(has_extra))
    def _():
        wait_bytes(pack.at[:EXTRA], in_send.at[2])
        wait_bytes(gpack.at[:EXTRA], g_send.at[2])

    store.wait()


def hand_out(grads, dq, dk, dv, sems):
    stores = [
        pltpu.make_async_copy(grads.at[a], ref.at[0], sems.at[a])
        for a, ref in enumerate((dq, dk, dv))
    ]
    for store in stores:
        store.start()
    for store in stores:
        store.wait()


def on_device(query_rows, key_rows, value_rows, handoff):
    shape = (ROWS, 2 * SIDE)
    dma = pltpu.SemaphoreType.DMA
    grads = pl.pallas_call(
        kernel,
        out_shape=pltpu.VMEM((3, *shape), BF16),
        in_specs=[pl.BlockSpec(memory_space=pl.ANY)] * 4,
        out_specs=pl.BlockSpec(memory_space=pl.ANY),
        scratch_shapes=[
            pltpu.VMEM((ROWS, SIDE), BF16),
            pltpu.VMEM((2, ROWS, SIDE), BF16),
            pltpu.VMEM((2, ROWS, SIDE), BF16),
            pltpu.VMEM((ROWS, SIDE), BF16),
            pltpu.VMEM((3, ROWS, SIDE), BF16),
            pltpu.VMEM((ROWS, SIDE), BF16),
            pltpu.VMEM((UNITS, 3, UNIT, HEAD), BF16),
            pltpu.VMEM((UNITS, UNIT, HEAD), BF16),
            pltpu.VMEM((3, CHIPS, 3, UNIT, HEAD), BF16),
            pltpu.VMEM((3, CHIPS, UNIT, HEAD), BF16),
            pltpu.VMEM((3, CHIPS, 3, UNIT, HEAD), BF16),
            pltpu.VMEM((2, ROWS, SIDE), F32),
            pltpu.VMEM((2, ROWS, SIDE), BF16),
            pltpu.VMEM((2, ROWS, SIDE), BF16),
            pltpu.VMEM((2, CHIPS * UNIT, HEAD), F32),
            pltpu.VMEM((3, ROWS, SIDE), BF16),
            dma((6,)),
            dma((2,)),
            dma((2,)),
            dma((2,)),
            dma((2,)),
            dma(()),
            dma(()),
            dma((3,)),
            dma((3,)),
            dma((3,)),
            dma((3,)),
            dma((3,)),
            dma((3,)),
            dma(()),
        ],
        compiler_params=pltpu.CompilerParams(
            collective_id=0, has_side_effects=True, vmem_limit_bytes=40 * 2**20
        ),
        name="space_time_backward",
    )(*(pltpu.with_memory_space_constraint(x[0], pltpu.HBM) for x in (query_rows, key_rows, value_rows, handoff)))
    results = pl.pallas_call(
        hand_out,
        out_shape=[jax.ShapeDtypeStruct((1, *shape), BF16)] * 3,
        in_specs=[pl.BlockSpec(memory_space=pl.ANY)],
        out_specs=[pl.BlockSpec(memory_space=pl.ANY)] * 3,
        scratch_shapes=[dma((3,))],
        compiler_params=pltpu.CompilerParams(vmem_limit_bytes=16 * 2**20),
        name="hand_out",
    )(pltpu.with_memory_space_constraint(grads, pltpu.VMEM))
    return tuple(results)


def solution(mesh):
    spec = P("segment", "seq", None)
    return jax.shard_map(
        on_device, mesh=mesh, in_specs=(spec,) * 4, out_specs=(spec,) * 3, check_vma=False
    )
```

```python
import jax
import jax.numpy as jnp
from jax import lax
from jax.experimental import pallas as pl
from jax.experimental.pallas import tpu as pltpu
from jax.sharding import PartitionSpec as P

MESH = pl.DeviceIdType.MESH
HEAD = 128
HALF = 6
ROWS = 192
SIDE = HALF * HEAD
UNIT = 16
CHIPS = 32
RING = 16
UNITS = ROWS // UNIT * HALF
EXTRA = UNITS - 2 * CHIPS
SCALE = HEAD**-0.5
AHEAD = 24
BF16, F32 = jnp.bfloat16, jnp.float32


def dot_nt(a, b):
    return lax.dot_general(a, b, (((1,), (1,)), ((), ())), preferred_element_type=F32)


def dot_tn(a, b):
    return lax.dot_general(a, b, (((0,), (0,)), ((), ())), preferred_element_type=F32)


def dot_nn(a, b):
    return lax.dot_general(a, b, (((1,), (0,)), ((), ())), preferred_element_type=F32)


def attention_backward(q, k, v, g, mask):
    scores = dot_nt(q, k) * SCALE
    if mask is not None:
        scores = jnp.where(mask, scores, -jnp.inf)
    top = jnp.max(scores, axis=1, keepdims=True)
    raised = jnp.exp(scores - top)
    weights = raised * (1.0 / jnp.sum(raised, axis=1, keepdims=True))
    low = weights.astype(BF16)
    grad_weights = dot_nt(g, v)
    delta = jnp.sum(low.astype(F32) * grad_weights, axis=1, keepdims=True)
    grad_scores = (weights * (grad_weights - delta)).astype(BF16)
    dq = dot_nn(grad_scores, k) * SCALE
    dk = dot_tn(grad_scores, q) * SCALE
    dv = dot_tn(low, g)
    return dq, dk, dv


def kernel(
    q_hbm, k_hbm, v_hbm, h_hbm, grads,
    qs, kb, vb, gs, xt, gt, pack, gpack, inb, ing, outb, own, sib_out, sib_in, acc, stage,
    load_sem, hand_send, hand_recv, pair_send, pair_recv, back_send, back_recv,
    in_send, in_recv, g_send, g_recv, out_send, out_recv, store_sem,
):
    seg = lax.axis_index("segment")
    me = lax.axis_index("seq")
    core = me % 2
    chip = me // 2
    z, xl = chip % RING, chip // RING
    sections = lax.axis_size("segment")
    seg_up = (seg + 1) % sections
    seg_down = (seg + sections - 1) % sections
    sibling = chip * 2 + (1 - core)
    has_extra = z % 4 == 1 + 2 * core
    extra_slot = xl * 4 + z // 4

    def chip_at(o):
        dx, step = o % 2, o // 2
        dz = jnp.where(step % 2 == 1, (step + 1) // 2, RING - step // 2)
        return ((xl + dx) % 2) * RING + (z + dz) % RING

    loads = []
    for a, ref in enumerate((q_hbm, k_hbm, v_hbm)):
        loads.append(pltpu.make_async_copy(ref.at[:, SIDE:], xt.at[a], load_sem.at[a]))
    loads.append(pltpu.make_async_copy(k_hbm.at[:, :SIDE], kb.at[0], load_sem.at[3]))
    loads.append(pltpu.make_async_copy(v_hbm.at[:, :SIDE], vb.at[0], load_sem.at[4]))
    loads.append(pltpu.make_async_copy(q_hbm.at[:, :SIDE], qs, load_sem.at[5]))
    for load in loads[:3]:
        load.start()

    barrier = pltpu.get_barrier_semaphore()

    def greet(i, carry):
        pl.semaphore_signal(
            barrier, inc=1, device_id={"seq": chip_at(CHIPS - i) * 2 + core}, device_id_type=MESH
        )
        return carry

    lax.fori_loop(1, CHIPS, greet, 0, unroll=True)
    pl.semaphore_signal(barrier, inc=1, device_id={"segment": seg_up}, device_id_type=MESH)
    pl.semaphore_signal(barrier, inc=1, device_id={"seq": sibling}, device_id_type=MESH)
    for load in loads[3:]:
        load.start()

    for load in loads[:3]:
        load.wait()
    for n in range(UNITS):
        rows = slice(n // HALF * UNIT, (n // HALF + 1) * UNIT)
        cols = slice(n % HALF * HEAD, (n % HALF + 1) * HEAD)
        for a in range(3):
            pack[n, a] = xt[a, rows, cols]
    for load in loads[3:]:
        load.wait()

    pl.semaphore_wait(barrier, CHIPS + 1)

    hand_t = pltpu.make_async_remote_copy(
        h_hbm.at[:, SIDE:], gt, hand_send.at[0], hand_recv.at[0],
        device_id={"segment": seg_down}, device_id_type=MESH,
    )
    hand_s = pltpu.make_async_remote_copy(
        h_hbm.at[:, :SIDE], gs, hand_send.at[1], hand_recv.at[1],
        device_id={"segment": seg_down}, device_id_type=MESH,
    )
    hand_t.start()

    def keep_in(u, source, landing, recv):
        pltpu.make_async_copy(source.at[u * CHIPS + chip], landing.at[u, chip], recv.at[u]).start()

    def send_in(u, source, landing, send, recv, first=1, last=CHIPS):
        def one(o, carry):
            j = chip_at(o)
            pltpu.make_async_remote_copy(
                source.at[u * CHIPS + j], landing.at[u, chip], send.at[u], recv.at[u],
                device_id={"seq": j * 2 + core}, device_id_type=MESH,
            ).start()
            return carry

        lax.fori_loop(first, last, one, 0)

    def send_extra(source, landing, send, recv):
        def one(i, carry):
            col, quarter = i % 2, (z // 4 + i // 2) % 4
            j = col * RING + quarter * 4 + 1 + 2 * core
            slot = 2 * CHIPS + col * 4 + quarter

            @pl.when(j != chip)
            def _():
                pltpu.make_async_remote_copy(
                    source.at[slot], landing.at[2, chip], send.at[2], recv.at[2],
                    device_id={"seq": j * 2 + core}, device_id_type=MESH,
                ).start()

            @pl.when(j == chip)
            def _():
                pltpu.make_async_copy(source.at[slot], landing.at[2, chip], recv.at[2]).start()

            return carry

        lax.fori_loop(0, EXTRA, one, 0)

    def wait_bytes(ref, sem):
        pltpu.make_async_copy(ref, ref, sem).wait()

    for u in range(2):
        keep_in(u, pack, inb, in_recv)
    ahead = jnp.where(core == 0, CHIPS, AHEAD)
    send_in(0, pack, inb, in_send, in_recv, last=ahead)

    pair = []
    for a, buf in enumerate((kb, vb)):
        pair.append(
            pltpu.make_async_remote_copy(
                buf.at[0], buf.at[1], pair_send.at[a], pair_recv.at[a],
                device_id={"seq": sibling}, device_id_type=MESH,
            )
        )
        pair[-1].start()
    hand_s.start()

    hand_t.wait_recv()
    for n in range(UNITS):
        rows = slice(n // HALF * UNIT, (n // HALF + 1) * UNIT)
        cols = slice(n % HALF * HEAD, (n % HALF + 1) * HEAD)
        gpack[n] = gt[rows, cols]
    for u in range(2):
        keep_in(u, gpack, ing, g_recv)
    send_in(0, pack, inb, in_send, in_recv, first=ahead)
    send_in(0, gpack, ing, g_send, g_recv)
    send_in(1, pack, inb, in_send, in_recv)
    send_in(1, gpack, ing, g_send, g_recv)
    send_extra(pack, inb, in_send, in_recv)
    send_extra(gpack, ing, g_send, g_recv)

    hand_s.wait_recv()
    for copy in pair:
        copy.wait_recv()

    for h in range(HALF):
        cols = slice(h * HEAD, (h + 1) * HEAD)
        k = kb[:, :, cols].reshape(2 * ROWS, HEAD)
        v = vb[:, :, cols].reshape(2 * ROWS, HEAD)
        dq, dk, dv = attention_backward(qs[:, cols], k, v, gs[:, cols], None)
        stage[0, :, cols] = dq.astype(BF16)
        own[0, :, cols] = dk[:ROWS]
        own[1, :, cols] = dv[:ROWS]
        sib_out[0, :, cols] = dk[ROWS:].astype(BF16)
        sib_out[1, :, cols] = dv[ROWS:].astype(BF16)
    back = pltpu.make_async_remote_copy(
        sib_out, sib_in, back_send, back_recv, device_id={"seq": sibling}, device_id_type=MESH
    )
    back.start()

    def temporal(u):
        wait_bytes(inb.at[u], in_recv.at[u])
        wait_bytes(ing.at[u], g_recv.at[u])
        k = inb[u, :, 1].reshape(CHIPS * UNIT, HEAD)
        v = inb[u, :, 2].reshape(CHIPS * UNIT, HEAD)
        part = CHIPS // 2
        row = lax.broadcasted_iota(jnp.int32, (part * UNIT, CHIPS * UNIT), 0)
        column = lax.broadcasted_iota(jnp.int32, (part * UNIT, CHIPS * UNIT), 1)
        mask = row % UNIT == column % UNIT
        for c in range(2):
            frames = slice(c * part, (c + 1) * part)
            q = inb[u, frames, 0].reshape(part * UNIT, HEAD)
            g = ing[u, frames].reshape(part * UNIT, HEAD)
            dq, dk, dv = attention_backward(q, k, v, g, mask)
            outb[u, frames, 0] = dq.astype(BF16).reshape(part, UNIT, HEAD)
            if c == 0:
                acc[0] = dk
                acc[1] = dv
            else:
                outb[u, :, 1] = (acc[0] + dk).astype(BF16).reshape(CHIPS, UNIT, HEAD)
                outb[u, :, 2] = (acc[1] + dv).astype(BF16).reshape(CHIPS, UNIT, HEAD)

        pltpu.make_async_copy(outb.at[u, chip], home(u), out_recv.at[u]).start()

    def home(u):
        n = jnp.where(u < 2, u * CHIPS + chip, 2 * CHIPS + extra_slot)
        rows = pl.ds(pl.multiple_of(n // HALF * UNIT, UNIT), UNIT)
        cols = pl.ds(pl.multiple_of(SIDE + n % HALF * HEAD, HEAD), HEAD)
        return grads.at[:, rows, cols]

    def send_out(u, base, count):
        landing = home(u)

        def one(i, carry):
            j = (xl + i) % 2 * RING + base + (z + i // 2) % count

            @pl.when(j != chip)
            def _():
                pltpu.make_async_remote_copy(
                    outb.at[u, j], landing, out_send.at[u], out_recv.at[u],
                    device_id={"seq": j * 2 + core}, device_id_type=MESH,
                ).start()

            return carry

        lax.fori_loop(0, 2 * count, one, 0)

    early, middle, late = (0, 4), (4, 4), (8, 8)
    temporal(0)
    for where in (early, middle, late):
        send_out(0, *where)
    temporal(1)
    send_out(1, *early)

    @pl.when(has_extra)
    def _():
        temporal(2)
        send_out(2, *early)

    send_out(1, *middle)

    @pl.when(has_extra)
    def _():
        send_out(2, *middle)

    send_out(1, *late)

    @pl.when(has_extra)
    def _():
        send_out(2, *late)

    back.wait_recv()
    for a in range(2):
        stage[1 + a] = (own[a] + sib_in[a].astype(F32)).astype(BF16)
    store = pltpu.make_async_copy(stage, grads.at[:, :, :SIDE], store_sem)
    store.start()

    for u in range(2):
        wait_bytes(outb.at[0], out_recv.at[u])
    wait_bytes(outb.at[0, :EXTRA], out_recv.at[2])

    hand_t.wait_send()
    hand_s.wait_send()
    for copy in pair:
        copy.wait_send()
    back.wait_send()
    for u in range(2):
        wait_bytes(pack.at[: CHIPS - 1], in_send.at[u])
        wait_bytes(gpack.at[: CHIPS - 1], g_send.at[u])
        wait_bytes(outb.at[0, : CHIPS - 1], out_send.at[u])

    @pl.when(has_extra)
    def _():
        wait_bytes(pack.at[: EXTRA - 1], in_send.at[2])
        wait_bytes(gpack.at[: EXTRA - 1], g_send.at[2])
        wait_bytes(outb.at[0, : CHIPS - 1], out_send.at[2])

    @pl.when(jnp.logical_not(has_extra))
    def _():
        wait_bytes(pack.at[:EXTRA], in_send.at[2])
        wait_bytes(gpack.at[:EXTRA], g_send.at[2])

    store.wait()


def hand_out(grads, dq, dk, dv, sems):
    stores = [
        pltpu.make_async_copy(grads.at[a], ref.at[0], sems.at[a])
        for a, ref in enumerate((dq, dk, dv))
    ]
    for store in stores:
        store.start()
    for store in stores:
        store.wait()


def on_device(query_rows, key_rows, value_rows, handoff):
    shape = (ROWS, 2 * SIDE)
    dma = pltpu.SemaphoreType.DMA
    grads = pl.pallas_call(
        kernel,
        out_shape=pltpu.VMEM((3, *shape), BF16),
        in_specs=[pl.BlockSpec(memory_space=pl.ANY)] * 4,
        out_specs=pl.BlockSpec(memory_space=pl.ANY),
        scratch_shapes=[
            pltpu.VMEM((ROWS, SIDE), BF16),
            pltpu.VMEM((2, ROWS, SIDE), BF16),
            pltpu.VMEM((2, ROWS, SIDE), BF16),
            pltpu.VMEM((ROWS, SIDE), BF16),
            pltpu.VMEM((3, ROWS, SIDE), BF16),
            pltpu.VMEM((ROWS, SIDE), BF16),
            pltpu.VMEM((UNITS, 3, UNIT, HEAD), BF16),
            pltpu.VMEM((UNITS, UNIT, HEAD), BF16),
            pltpu.VMEM((3, CHIPS, 3, UNIT, HEAD), BF16),
            pltpu.VMEM((3, CHIPS, UNIT, HEAD), BF16),
            pltpu.VMEM((3, CHIPS, 3, UNIT, HEAD), BF16),
            pltpu.VMEM((2, ROWS, SIDE), F32),
            pltpu.VMEM((2, ROWS, SIDE), BF16),
            pltpu.VMEM((2, ROWS, SIDE), BF16),
            pltpu.VMEM((2, CHIPS * UNIT, HEAD), F32),
            pltpu.VMEM((3, ROWS, SIDE), BF16),
            dma((6,)),
            dma((2,)),
            dma((2,)),
            dma((2,)),
            dma((2,)),
            dma(()),
            dma(()),
            dma((3,)),
            dma((3,)),
            dma((3,)),
            dma((3,)),
            dma((3,)),
            dma((3,)),
            dma(()),
        ],
        compiler_params=pltpu.CompilerParams(
            collective_id=0, has_side_effects=True, vmem_limit_bytes=40 * 2**20
        ),
        name="space_time_backward",
    )(*(pltpu.with_memory_space_constraint(x[0], pltpu.HBM) for x in (query_rows, key_rows, value_rows, handoff)))
    results = pl.pallas_call(
        hand_out,
        out_shape=[jax.ShapeDtypeStruct((1, *shape), BF16)] * 3,
        in_specs=[pl.BlockSpec(memory_space=pl.ANY)],
        out_specs=[pl.BlockSpec(memory_space=pl.ANY)] * 3,
        scratch_shapes=[dma((3,))],
        compiler_params=pltpu.CompilerParams(vmem_limit_bytes=16 * 2**20),
        name="hand_out",
    )(pltpu.with_memory_space_constraint(grads, pltpu.VMEM))
    return tuple(results)


def solution(mesh):
    spec = P("segment", "seq", None)
    return jax.shard_map(
        on_device, mesh=mesh, in_specs=(spec,) * 4, out_specs=(spec,) * 3, check_vma=False
    )
```

```python
import jax
import jax.numpy as jnp
from jax import lax
from jax.experimental import pallas as pl
from jax.experimental.pallas import tpu as pltpu
from jax.sharding import PartitionSpec as P

MESH = pl.DeviceIdType.MESH
HEAD = 128
HALF = 6
ROWS = 192
SIDE = HALF * HEAD
UNIT = 16
CHIPS = 32
RING = 16
UNITS = ROWS // UNIT * HALF
EXTRA = UNITS - 2 * CHIPS
SCALE = HEAD**-0.5
AHEAD = 24
BF16, F32 = jnp.bfloat16, jnp.float32


def dot_nt(a, b):
    return lax.dot_general(a, b, (((1,), (1,)), ((), ())), preferred_element_type=F32)


def dot_tn(a, b):
    return lax.dot_general(a, b, (((0,), (0,)), ((), ())), preferred_element_type=F32)


def dot_nn(a, b):
    return lax.dot_general(a, b, (((1,), (0,)), ((), ())), preferred_element_type=F32)


def attention_backward(q, k, v, g, mask):
    scores = dot_nt(q, k) * SCALE
    if mask is not None:
        scores = jnp.where(mask, scores, -jnp.inf)
    top = jnp.max(scores, axis=1, keepdims=True)
    raised = jnp.exp(scores - top)
    weights = raised * (1.0 / jnp.sum(raised, axis=1, keepdims=True))
    low = weights.astype(BF16)
    grad_weights = dot_nt(g, v)
    delta = jnp.sum(low.astype(F32) * grad_weights, axis=1, keepdims=True)
    grad_scores = (weights * (grad_weights - delta)).astype(BF16)
    dq = dot_nn(grad_scores, k) * SCALE
    dk = dot_tn(grad_scores, q) * SCALE
    dv = dot_tn(low, g)
    return dq, dk, dv


def kernel(
    q_hbm, k_hbm, v_hbm, h_hbm, grads,
    qs, kb, vb, gs, xt, gt, pack, gpack, inb, ing, outb, own, sib_out, sib_in, acc, stage,
    load_sem, hand_send, hand_recv, pair_send, pair_recv, back_send, back_recv,
    in_send, in_recv, g_send, g_recv, out_send, out_recv, store_sem,
):
    seg = lax.axis_index("segment")
    me = lax.axis_index("seq")
    core = me % 2
    chip = me // 2
    z, xl = chip % RING, chip // RING
    sections = lax.axis_size("segment")
    seg_up = (seg + 1) % sections
    seg_down = (seg + sections - 1) % sections
    sibling = chip * 2 + (1 - core)
    has_extra = z % 4 == 1 + 2 * core
    extra_slot = xl * 4 + z // 4

    def chip_at(o):
        dx, step = o % 2, o // 2
        dz = jnp.where(step % 2 == 1, (step + 1) // 2, RING - step // 2)
        return ((xl + dx) % 2) * RING + (z + dz) % RING

    loads = []
    for a, ref in enumerate((q_hbm, k_hbm, v_hbm)):
        loads.append(pltpu.make_async_copy(ref.at[:, SIDE:], xt.at[a], load_sem.at[a]))
    loads.append(pltpu.make_async_copy(k_hbm.at[:, :SIDE], kb.at[0], load_sem.at[3]))
    loads.append(pltpu.make_async_copy(v_hbm.at[:, :SIDE], vb.at[0], load_sem.at[4]))
    loads.append(pltpu.make_async_copy(q_hbm.at[:, :SIDE], qs, load_sem.at[5]))
    for load in loads[:3]:
        load.start()

    barrier = pltpu.get_barrier_semaphore()

    def greet(i, carry):
        pl.semaphore_signal(
            barrier, inc=1, device_id={"seq": chip_at(CHIPS - i) * 2 + core}, device_id_type=MESH
        )
        return carry

    lax.fori_loop(1, CHIPS, greet, 0, unroll=True)
    pl.semaphore_signal(barrier, inc=1, device_id={"segment": seg_up}, device_id_type=MESH)
    pl.semaphore_signal(barrier, inc=1, device_id={"seq": sibling}, device_id_type=MESH)
    for load in loads[3:]:
        load.start()

    for load in loads[:3]:
        load.wait()
    for n in range(UNITS):
        rows = slice(n // HALF * UNIT, (n // HALF + 1) * UNIT)
        cols = slice(n % HALF * HEAD, (n % HALF + 1) * HEAD)
        for a in range(3):
            pack[n, a] = xt[a, rows, cols]
    pl.semaphore_wait(barrier, CHIPS + 1)

    hand_t = pltpu.make_async_remote_copy(
        h_hbm.at[:, SIDE:], gt, hand_send.at[0], hand_recv.at[0],
        device_id={"segment": seg_down}, device_id_type=MESH,
    )
    hand_s = pltpu.make_async_remote_copy(
        h_hbm.at[:, :SIDE], gs, hand_send.at[1], hand_recv.at[1],
        device_id={"segment": seg_down}, device_id_type=MESH,
    )
    hand_t.start()

    def keep_in(u, source, landing, recv):
        pltpu.make_async_copy(source.at[u * CHIPS + chip], landing.at[u, chip], recv.at[u]).start()

    def send_in(u, source, landing, send, recv, first=1, last=CHIPS):
        def one(o, carry):
            j = chip_at(o)
            pltpu.make_async_remote_copy(
                source.at[u * CHIPS + j], landing.at[u, chip], send.at[u], recv.at[u],
                device_id={"seq": j * 2 + core}, device_id_type=MESH,
            ).start()
            return carry

        lax.fori_loop(first, last, one, 0)

    def send_extra(source, landing, send, recv):
        def one(i, carry):
            col, quarter = i % 2, (z // 4 + i // 2) % 4
            j = col * RING + quarter * 4 + 1 + 2 * core
            slot = 2 * CHIPS + col * 4 + quarter

            @pl.when(j != chip)
            def _():
                pltpu.make_async_remote_copy(
                    source.at[slot], landing.at[2, chip], send.at[2], recv.at[2],
                    device_id={"seq": j * 2 + core}, device_id_type=MESH,
                ).start()

            @pl.when(j == chip)
            def _():
                pltpu.make_async_copy(source.at[slot], landing.at[2, chip], recv.at[2]).start()

            return carry

        lax.fori_loop(0, EXTRA, one, 0)

    def wait_bytes(ref, sem):
        pltpu.make_async_copy(ref, ref, sem).wait()

    for u in range(2):
        keep_in(u, pack, inb, in_recv)
    ahead = jnp.where(core == 0, CHIPS, AHEAD)
    send_in(0, pack, inb, in_send, in_recv, last=ahead)

    for load in loads[3:]:
        load.wait()
    pair = []
    for a, buf in enumerate((kb, vb)):
        pair.append(
            pltpu.make_async_remote_copy(
                buf.at[0], buf.at[1], pair_send.at[a], pair_recv.at[a],
                device_id={"seq": sibling}, device_id_type=MESH,
            )
        )
        pair[-1].start()
    hand_s.start()

    hand_t.wait_recv()
    for n in range(UNITS):
        rows = slice(n // HALF * UNIT, (n // HALF + 1) * UNIT)
        cols = slice(n % HALF * HEAD, (n % HALF + 1) * HEAD)
        gpack[n] = gt[rows, cols]
    for u in range(2):
        keep_in(u, gpack, ing, g_recv)
    send_in(0, pack, inb, in_send, in_recv, first=ahead)
    send_in(0, gpack, ing, g_send, g_recv)
    send_in(1, pack, inb, in_send, in_recv)
    send_in(1, gpack, ing, g_send, g_recv)
    send_extra(pack, inb, in_send, in_recv)
    send_extra(gpack, ing, g_send, g_recv)

    hand_s.wait_recv()
    for copy in pair:
        copy.wait_recv()

    for h in range(HALF):
        cols = slice(h * HEAD, (h + 1) * HEAD)
        k = kb[:, :, cols].reshape(2 * ROWS, HEAD)
        v = vb[:, :, cols].reshape(2 * ROWS, HEAD)
        dq, dk, dv = attention_backward(qs[:, cols], k, v, gs[:, cols], None)
        stage[0, :, cols] = dq.astype(BF16)
        own[0, :, cols] = dk[:ROWS]
        own[1, :, cols] = dv[:ROWS]
        sib_out[0, :, cols] = dk[ROWS:].astype(BF16)
        sib_out[1, :, cols] = dv[ROWS:].astype(BF16)
    back = pltpu.make_async_remote_copy(
        sib_out, sib_in, back_send, back_recv, device_id={"seq": sibling}, device_id_type=MESH
    )
    back.start()

    def temporal(u):
        wait_bytes(inb.at[u], in_recv.at[u])
        wait_bytes(ing.at[u], g_recv.at[u])
        k = inb[u, :, 1].reshape(CHIPS * UNIT, HEAD)
        v = inb[u, :, 2].reshape(CHIPS * UNIT, HEAD)
        part = CHIPS // 2
        row = lax.broadcasted_iota(jnp.int32, (part * UNIT, CHIPS * UNIT), 0)
        column = lax.broadcasted_iota(jnp.int32, (part * UNIT, CHIPS * UNIT), 1)
        mask = row % UNIT == column % UNIT
        for c in range(2):
            frames = slice(c * part, (c + 1) * part)
            q = inb[u, frames, 0].reshape(part * UNIT, HEAD)
            g = ing[u, frames].reshape(part * UNIT, HEAD)
            dq, dk, dv = attention_backward(q, k, v, g, mask)
            outb[u, frames, 0] = dq.astype(BF16).reshape(part, UNIT, HEAD)
            if c == 0:
                acc[0] = dk
                acc[1] = dv
            else:
                outb[u, :, 1] = (acc[0] + dk).astype(BF16).reshape(CHIPS, UNIT, HEAD)
                outb[u, :, 2] = (acc[1] + dv).astype(BF16).reshape(CHIPS, UNIT, HEAD)

        pltpu.make_async_copy(outb.at[u, chip], home(u), out_recv.at[u]).start()

    def home(u):
        n = jnp.where(u < 2, u * CHIPS + chip, 2 * CHIPS + extra_slot)
        rows = pl.ds(pl.multiple_of(n // HALF * UNIT, UNIT), UNIT)
        cols = pl.ds(pl.multiple_of(SIDE + n % HALF * HEAD, HEAD), HEAD)
        return grads.at[:, rows, cols]

    def send_out(u, base, count):
        landing = home(u)

        def one(i, carry):
            j = (xl + i) % 2 * RING + base + (z + i // 2) % count

            @pl.when(j != chip)
            def _():
                pltpu.make_async_remote_copy(
                    outb.at[u, j], landing, out_send.at[u], out_recv.at[u],
                    device_id={"seq": j * 2 + core}, device_id_type=MESH,
                ).start()

            return carry

        lax.fori_loop(0, 2 * count, one, 0)

    early, middle, late = (0, 4), (4, 4), (8, 8)
    temporal(0)
    for where in (early, middle, late):
        send_out(0, *where)
    temporal(1)
    send_out(1, *early)

    @pl.when(has_extra)
    def _():
        temporal(2)
        send_out(2, *early)

    send_out(1, *middle)

    @pl.when(has_extra)
    def _():
        send_out(2, *middle)

    send_out(1, *late)

    @pl.when(has_extra)
    def _():
        send_out(2, *late)

    back.wait_recv()
    for a in range(2):
        stage[1 + a] = (own[a] + sib_in[a].astype(F32)).astype(BF16)
    store = pltpu.make_async_copy(stage, grads.at[:, :, :SIDE], store_sem)
    store.start()

    for u in range(2):
        wait_bytes(outb.at[0], out_recv.at[u])
    wait_bytes(outb.at[0, :EXTRA], out_recv.at[2])

    hand_t.wait_send()
    hand_s.wait_send()
    for copy in pair:
        copy.wait_send()
    back.wait_send()
    for u in range(2):
        wait_bytes(pack.at[: CHIPS - 1], in_send.at[u])
        wait_bytes(gpack.at[: CHIPS - 1], g_send.at[u])
        wait_bytes(outb.at[0, : CHIPS - 1], out_send.at[u])

    @pl.when(has_extra)
    def _():
        wait_bytes(pack.at[: EXTRA - 1], in_send.at[2])
        wait_bytes(gpack.at[: EXTRA - 1], g_send.at[2])
        wait_bytes(outb.at[0, : CHIPS - 1], out_send.at[2])

    @pl.when(jnp.logical_not(has_extra))
    def _():
        wait_bytes(pack.at[:EXTRA], in_send.at[2])
        wait_bytes(gpack.at[:EXTRA], g_send.at[2])

    store.wait()


def hand_out(grads, dq, dk, dv, sems):
    stores = [
        pltpu.make_async_copy(grads.at[a], ref.at[0], sems.at[a])
        for a, ref in enumerate((dq, dk, dv))
    ]
    for store in stores:
        store.start()
    for store in stores:
        store.wait()


def on_device(query_rows, key_rows, value_rows, handoff):
    shape = (ROWS, 2 * SIDE)
    dma = pltpu.SemaphoreType.DMA
    grads = pl.pallas_call(
        kernel,
        out_shape=pltpu.VMEM((3, *shape), BF16),
        in_specs=[pl.BlockSpec(memory_space=pl.ANY)] * 4,
        out_specs=pl.BlockSpec(memory_space=pl.ANY),
        scratch_shapes=[
            pltpu.VMEM((ROWS, SIDE), BF16),
            pltpu.VMEM((2, ROWS, SIDE), BF16),
            pltpu.VMEM((2, ROWS, SIDE), BF16),
            pltpu.VMEM((ROWS, SIDE), BF16),
            pltpu.VMEM((3, ROWS, SIDE), BF16),
            pltpu.VMEM((ROWS, SIDE), BF16),
            pltpu.VMEM((UNITS, 3, UNIT, HEAD), BF16),
            pltpu.VMEM((UNITS, UNIT, HEAD), BF16),
            pltpu.VMEM((3, CHIPS, 3, UNIT, HEAD), BF16),
            pltpu.VMEM((3, CHIPS, UNIT, HEAD), BF16),
            pltpu.VMEM((3, CHIPS, 3, UNIT, HEAD), BF16),
            pltpu.VMEM((2, ROWS, SIDE), F32),
            pltpu.VMEM((2, ROWS, SIDE), BF16),
            pltpu.VMEM((2, ROWS, SIDE), BF16),
            pltpu.VMEM((2, CHIPS * UNIT, HEAD), F32),
            pltpu.VMEM((3, ROWS, SIDE), BF16),
            dma((6,)),
            dma((2,)),
            dma((2,)),
            dma((2,)),
            dma((2,)),
            dma(()),
            dma(()),
            dma((3,)),
            dma((3,)),
            dma((3,)),
            dma((3,)),
            dma((3,)),
            dma((3,)),
            dma(()),
        ],
        compiler_params=pltpu.CompilerParams(
            collective_id=0, has_side_effects=True, vmem_limit_bytes=40 * 2**20
        ),
        name="space_time_backward",
    )(*(pltpu.with_memory_space_constraint(x[0], pltpu.HBM) for x in (query_rows, key_rows, value_rows, handoff)))
    results = pl.pallas_call(
        hand_out,
        out_shape=[jax.ShapeDtypeStruct((1, *shape), BF16)] * 3,
        in_specs=[pl.BlockSpec(memory_space=pl.ANY)],
        out_specs=[pl.BlockSpec(memory_space=pl.ANY)] * 3,
        scratch_shapes=[dma((3,))],
        compiler_params=pltpu.CompilerParams(vmem_limit_bytes=16 * 2**20),
        name="hand_out",
    )(pltpu.with_memory_space_constraint(grads, pltpu.VMEM))
    return tuple(results)


def solution(mesh):
    spec = P("segment", "seq", None)
    return jax.shard_map(
        on_device, mesh=mesh, in_specs=(spec,) * 4, out_specs=(spec,) * 3, check_vma=False
    )
```
